32 devices in a mesh: grp: 2 (over y), gy: 4 (over z), gz: 4 (over x, core).
Axes of the slice: x: 2, y: 2, z: 4, core: 2. Of those that a mesh axis runs over, the one named last changes fastest.
Arguments:
- snapshots: bfloat16 [512, 8, 16, 128], P('grp', 'gy', 'gz'), parts along dimension 0, may hold values from -12.5 to 12.5
- fluid_mask: int32 [16, 16, 128], P(('grp', 'gy'), 'gz'), parts along dimension 0, may hold values 0 or 1
Outputs:
- modes: float32 [512, 8, 16, 128], P('grp', 'gy', 'gz'), parts along dimension 0
- factor: float32 [512, 256], P('grp'), parts along dimension 0
The draws below stay inside these ranges and needn't reach their ends.
There are 2 independent parts, one for each index of `grp`. The reference program is written for one: setup_inputs(seed, part) draws one part's arguments, and reference() takes and returns one part's arrays. A program takes and returns all parts, laid end to end along the dimension named above; each array names one. Nothing has to cross between parts.
All inputs are finite; a program needn't handle non-finite values. No bound on the sum of `fluid_mask` on one device may be relied on, other than what follows from the above.
Results may differ from the reference program's by a relative error of at most 0.0003.
Values may be sent and summed in bfloat16 or wider, within the bound.
A program may use at most 64 MiB of HBM per device.

```python
import math
import jax
import jax.numpy as jnp
from jax import lax

COLS = 256
NX = 128
NY = 8
NZ = 16


def draw_snapshots(key, part):
    common_key = jax.random.fold_in(key, 3)
    noise_key = jax.random.fold_in(key, 5)
    common = jnp.clip(jax.random.normal(common_key, (NY, NZ, NX), jnp.float32), -4.0, 4.0)
    noise = jnp.clip(jax.random.normal(noise_key, (COLS, NY, NZ, NX), jnp.float32), -4.0, 4.0)
    mixed = common[None] + 0.02 * noise
    profile = 1.0 + 2.0 * jnp.arange(NY, dtype=jnp.float32) / max(NY - 1, 1)
    mixed = mixed * profile.reshape(1, NY, 1, 1)
    return mixed.astype(jnp.bfloat16)


def with_ends(array, own_key, low, high):
    shape = array.shape
    index_at = [jax.random.randint(jax.random.fold_in(own_key, axis), (), 0, shape[axis]) for axis in range(len(shape))]
    array = array.at[tuple(index_at)].set(low)
    longest = shape.index(max(shape))
    index_at[longest] = (index_at[longest] + 1) % shape[longest]
    return array.at[tuple(index_at)].set(high)


def setup_inputs(seed: int = 0, part: int = 0) -> dict:
    streams_of = jax.random.split(jax.random.key(seed), 3)
    own_keys = jax.random.split(jax.random.fold_in(streams_of[2], part), 3)
    snapshots = draw_snapshots(jax.random.fold_in(jax.random.fold_in(streams_of[2], part), 71), part)
    fluid_mask = with_ends((jax.random.randint(own_keys[1], (NY, NZ, NX), 0, 4) < 3).astype(jnp.int32), jax.random.fold_in(own_keys[1], 1), 0, 1)
    return dict(snapshots=snapshots, fluid_mask=fluid_mask)


gauss_taps = (0.05448868, 0.24420134, 0.40261995, 0.24420134, 0.05448868)

def filter_inner(field, axis, length):
    total = gauss_taps[0] * lax.slice_in_dim(field, 0, length, axis=axis)
    for offset in range(1, 5):
        total = total + gauss_taps[offset] * lax.slice_in_dim(field, offset, offset + length, axis=axis)
    return total

def filter_edge(field, axis):
    widths = [(0, 0)] * field.ndim
    widths[axis] = (2, 2)
    return filter_inner(jnp.pad(field, widths), axis, field.shape[axis])

def cholesky_pair(gram):
    count = gram.shape[0]
    places = jnp.arange(count, dtype=jnp.int32)

    def column_step(index, carry):
        upper, inverse = carry
        index = jnp.asarray(index).astype(jnp.int32)
        column = lax.dynamic_slice_in_dim(upper, index, 1, 1)[:, 0]
        grow = lax.dynamic_slice_in_dim(gram, index, 1, 0)[0]
        rest = grow - jnp.dot(column, upper, precision=lax.Precision.HIGHEST)
        pick = (places == index).astype(jnp.float32)
        pivot = jnp.sqrt(jnp.sum(rest * pick))
        row_new = jnp.where(places >= index, rest, jnp.float32(0.0)) / pivot
        upper = upper + pick[:, None] * row_new[None, :]
        inv_col = (pick - jnp.dot(inverse, column, precision=lax.Precision.HIGHEST)) / pivot
        inverse = inverse + inv_col[:, None] * pick[None, :]
        return (upper, inverse)
    start = jnp.zeros((count, count), jnp.float32)
    return lax.fori_loop(0, count, column_step, (start, start))

def upper_factor(matrix):
    gram = jnp.dot(matrix, matrix.T, precision=lax.Precision.HIGHEST)
    return cholesky_pair(gram)

def reference(snapshots, fluid_mask):
    field = snapshots.astype(jnp.float32)
    field = filter_edge(field, 3)
    field = filter_edge(field, 1)
    field = filter_edge(field, 2)
    field = field * fluid_mask.astype(jnp.float32)[None]
    matrix = field.reshape(field.shape[0], -1)
    scale = math.sqrt(matrix.shape[1])
    first, first_inv = upper_factor(matrix)
    basis = jnp.dot(first_inv.T, matrix, precision=lax.Precision.HIGHEST)
    second, second_inv = upper_factor(basis)
    ortho = jnp.dot(second_inv.T, basis, precision=lax.Precision.HIGHEST)
    modes = (ortho * scale).reshape(snapshots.shape)
    factor = jnp.dot(second, first, precision=lax.Precision.HIGHEST) / scale
    return (modes, factor)
```

```python
import math

import jax
import jax.numpy as jnp
from jax import lax
from jax.experimental import pallas as pl
from jax.experimental.pallas import tpu as pltpu
from jax.sharding import PartitionSpec as P

gauss_taps = (0.05448868, 0.24420134, 0.40261995, 0.24420134, 0.05448868)


def with_halo(cells, sides, width):
    for axis, dim in sides:
        count = lax.axis_size(axis)
        ends = count - 1
        head = lax.slice_in_dim(cells, 0, width, axis=dim)
        tail = lax.slice_in_dim(cells, cells.shape[dim] - width, cells.shape[dim], axis=dim)
        cells = jnp.concatenate(
            [
                lax.ppermute(tail, axis, [(i, (i + 1) % count) for i in range(ends)]),
                cells,
                lax.ppermute(head, axis, [((i + 1) % count, i) for i in range(ends)]),
            ],
            axis=dim,
        )
    return cells


def filter_inner(field, axis, length):
    total = gauss_taps[0] * lax.slice_in_dim(field, 0, length, axis=axis)
    for offset in range(1, 5):
        total = total + gauss_taps[offset] * lax.slice_in_dim(
            field, offset, offset + length, axis=axis
        )
    return total


def filter_edge(field, axis):
    widths = [(0, 0)] * field.ndim
    widths[axis] = (2, 2)
    return filter_inner(jnp.pad(field, widths), axis, field.shape[axis])


def factor_block(block, vals, diag):
    count = block.shape[0]
    lanes = lax.broadcasted_iota(jnp.int32, (8, count), 1)
    subs = lax.broadcasted_iota(jnp.int32, (8, count), 0)
    wide = (8, count)
    tiles = [block[8 * t : 8 * t + 8] for t in range(count // 8)]
    for p in range(count // 8):
        base = 8 * p
        panel = tiles[p]
        rows = [jnp.broadcast_to(panel[k : k + 1], wide) for k in range(8)]
        a = [
            [jnp.broadcast_to(rows[i][:, base + k : base + k + 1], wide) for k in range(i + 1)]
            for i in range(8)
        ]
        inv = []
        m = [[None] * 8 for _ in range(8)]
        for k in range(8):
            inv.append(1.0 / a[k][k])
            for i in range(k + 1, 8):
                m[i][k] = a[i][k] * inv[k]
            for i in range(k + 1, 8):
                for l in range(k + 1, i + 1):
                    a[i][l] = a[i][l] - m[i][k] * a[l][k]
        here = [lanes == base + k for k in range(8)]
        solved = []
        ones = []
        for i in range(8):
            row = rows[i]
            for k in range(i):
                row = jnp.where(here[k], 0.0, row) - m[i][k] * ones[k]
            solved.append(row)
            ones.append(jnp.where(here[i], 1.0, row))
        out = solved[0]
        dia = a[0][0]
        for k in range(1, 8):
            out = jnp.where(subs == k, solved[k], out)
            dia = jnp.where(subs == k, a[k][k], dia)
        vals[base : base + 8] = out
        diag[base : base + 8] = dia
        inside = (lanes >= base) & (lanes < base + 8)
        past = [jnp.where(inside & (lanes > base + k), 0.0, ones[k]) for k in range(8)]
        for t in range(p + 1, count // 8):
            tile = tiles[t]
            q = []
            for k in range(8):
                c = jnp.broadcast_to(tile[:, base + k : base + k + 1], wide)
                for l in range(k):
                    c = c - q[l] * a[k][l]
                q.append(c * inv[k])
            tile = jnp.where(inside, 0.0, tile)
            for k in range(8):
                tile = tile - q[k] * past[k]
            tiles[t] = tile
    v = vals[...]
    d = diag[...]
    s = lax.rsqrt(d)
    s = s * (1.5 - 0.5 * d * s * s)
    v = v * s
    ri = lax.broadcasted_iota(jnp.int32, (count, count), 0)
    ci = lax.broadcasted_iota(jnp.int32, (count, count), 1)
    upper = jnp.where(ci >= ri, v, 0.0)
    lower = jnp.where(ci < ri, v, jnp.where(ci == ri, s, 0.0))
    return upper, lower


def hdot(a, b, ca=1, cb=0):
    return lax.dot_general(
        a, b, (((ca,), (cb,)), ((), ())), precision=lax.Precision.HIGHEST, preferred_element_type=jnp.float32
    )


def chol_kernel(g_ref, u_ref, l_ref, vals, diag):
    h = g_ref.shape[0] // 2
    u11, l11 = factor_block(g_ref[:h, :h], vals, diag)
    u12 = hdot(l11, g_ref[:h, h:])
    rest = g_ref[h:, h:] - hdot(u12, u12, 0, 0)
    u22, l22 = factor_block(rest, vals, diag)
    u_ref[:h, :h] = u11
    u_ref[:h, h:] = u12
    u_ref[h:, :h] = jnp.zeros((h, h), jnp.float32)
    u_ref[h:, h:] = u22
    l_ref[:h, :h] = l11
    l_ref[:h, h:] = jnp.zeros((h, h), jnp.float32)
    l_ref[h:, :h] = -hdot(l22, hdot(u12, l11, 0, 0))
    l_ref[h:, h:] = l22


def cholesky_pair(gram):
    n = gram.shape[0]
    sd = jax.ShapeDtypeStruct((n, n), jnp.float32)
    return pl.pallas_call(
        chol_kernel,
        out_shape=(sd, sd),
        in_specs=[pl.BlockSpec(memory_space=pltpu.VMEM)],
        out_specs=[pl.BlockSpec(memory_space=pltpu.VMEM)] * 2,
        scratch_shapes=[pltpu.VMEM((n // 2, n // 2), jnp.float32)] * 2,
    )(gram)


def total_factor(matrix):
    gram = jnp.dot(matrix, matrix.T, precision=lax.Precision.HIGHEST)
    summed = lax.psum(gram, ("gy", "gz"))
    return cholesky_pair(summed)


def body(snapshots, fluid_mask):
    cells_y = snapshots.shape[1]
    cells_z = snapshots.shape[2]
    extended = with_halo(snapshots, (("gy", 1),), 2)
    field = filter_inner(filter_edge(extended.astype(jnp.float32), 3), 1, cells_y)
    widened = with_halo(field, (("gz", 2),), 2)
    field = filter_inner(widened, 2, cells_z)
    field = field * fluid_mask.astype(jnp.float32)[None]
    matrix = field.reshape(field.shape[0], -1)
    scale = math.sqrt(matrix.shape[1] * lax.axis_size("gy") * lax.axis_size("gz"))
    first, first_inv = total_factor(matrix)
    basis = jnp.dot(first_inv, matrix, precision=lax.Precision.HIGHEST)
    second, second_inv = total_factor(basis)
    ortho = jnp.dot(second_inv, basis, precision=lax.Precision.HIGHEST)
    modes = (ortho * scale).reshape(snapshots.shape)
    factor = jnp.dot(second, first, precision=lax.Precision.HIGHEST) / scale
    return (modes, factor)


def solution(mesh):
    placed = (P("grp", "gy", "gz", None), P(("grp", "gy"), "gz", None))
    return jax.shard_map(
        body,
        mesh=mesh,
        in_specs=placed,
        out_specs=(P("grp", "gy", "gz", None), P("grp", None)),
        check_vma=False,
    )
```

```python
import functools
import math

import jax
import jax.numpy as jnp
from jax import lax
from jax.experimental import pallas as pl
from jax.experimental.pallas import tpu as pltpu
from jax.sharding import PartitionSpec as P

MESH = pl.DeviceIdType.MESH
VMEM = pl.BlockSpec(memory_space=pltpu.VMEM)
gauss_taps = (0.05448868, 0.24420134, 0.40261995, 0.24420134, 0.05448868)


def with_halo(cells, sides, width):
    for axis, dim in sides:
        count = lax.axis_size(axis)
        ends = count - 1
        head = lax.slice_in_dim(cells, 0, width, axis=dim)
        tail = lax.slice_in_dim(cells, cells.shape[dim] - width, cells.shape[dim], axis=dim)
        cells = jnp.concatenate(
            [
                lax.ppermute(tail, axis, [(i, (i + 1) % count) for i in range(ends)]),
                cells,
                lax.ppermute(head, axis, [((i + 1) % count, i) for i in range(ends)]),
            ],
            axis=dim,
        )
    return cells


def filter_inner(field, axis, length):
    total = gauss_taps[0] * lax.slice_in_dim(field, 0, length, axis=axis)
    for offset in range(1, 5):
        total = total + gauss_taps[offset] * lax.slice_in_dim(
            field, offset, offset + length, axis=axis
        )
    return total


def filter_edge(field, axis):
    widths = [(0, 0)] * field.ndim
    widths[axis] = (2, 2)
    return filter_inner(jnp.pad(field, widths), axis, field.shape[axis])


def hdot(a, b, ca=1, cb=0):
    return lax.dot_general(
        a,
        b,
        (((ca,), (cb,)), ((), ())),
        precision=lax.Precision.HIGHEST,
        preferred_element_type=jnp.float32,
    )


def factor_block(block, vals, diag):
    count = block.shape[0]
    lanes = lax.broadcasted_iota(jnp.int32, (8, count), 1)
    subs = lax.broadcasted_iota(jnp.int32, (8, count), 0)
    wide = (8, count)
    tiles = [block[8 * t : 8 * t + 8] for t in range(count // 8)]
    for p in range(count // 8):
        base = 8 * p
        panel = tiles[p]
        rows = [jnp.broadcast_to(panel[k : k + 1], wide) for k in range(8)]
        a = [
            [jnp.broadcast_to(rows[i][:, base + k : base + k + 1], wide) for k in range(i + 1)]
            for i in range(8)
        ]
        inv = []
        m = [[None] * 8 for _ in range(8)]
        for k in range(8):
            inv.append(1.0 / a[k][k])
            for i in range(k + 1, 8):
                m[i][k] = a[i][k] * inv[k]
            for i in range(k + 1, 8):
                for l in range(k + 1, i + 1):
                    a[i][l] = a[i][l] - m[i][k] * a[l][k]
        here = [lanes == base + k for k in range(8)]
        solved = []
        ones = []
        for i in range(8):
            row = rows[i]
            for k in range(i):
                row = jnp.where(here[k], 0.0, row) - m[i][k] * ones[k]
            solved.append(row)
            ones.append(jnp.where(here[i], 1.0, row))
        out = solved[0]
        dia = a[0][0]
        for k in range(1, 8):
            out = jnp.where(subs == k, solved[k], out)
            dia = jnp.where(subs == k, a[k][k], dia)
        vals[base : base + 8] = out
        diag[base : base + 8] = dia
        inside = (lanes >= base) & (lanes < base + 8)
        past = [jnp.where(inside & (lanes > base + k), 0.0, ones[k]) for k in range(8)]
        for t in range(p + 1, count // 8):
            tile = tiles[t]
            q = []
            for k in range(8):
                c = jnp.broadcast_to(tile[:, base + k : base + k + 1], wide)
                for l in range(k):
                    c = c - q[l] * a[k][l]
                q.append(c * inv[k])
            tile = jnp.where(inside, 0.0, tile)
            for k in range(8):
                tile = tile - q[k] * past[k]
            tiles[t] = tile
    v = vals[...]
    d = diag[...]
    s = lax.rsqrt(d)
    s = s * (1.5 - 0.5 * d * s * s)
    v = v * s
    ri = lax.broadcasted_iota(jnp.int32, (count, count), 0)
    ci = lax.broadcasted_iota(jnp.int32, (count, count), 1)
    upper = jnp.where(ci >= ri, v, 0.0)
    lower = jnp.where(ci < ri, v, jnp.where(ci == ri, s, 0.0))
    return upper, lower


def factor_packed(g_ref, u_ref, l_ref, vals, diag):
    h = g_ref.shape[1]
    u11, l11 = factor_block(g_ref[:h], vals, diag)
    u12 = hdot(l11, g_ref[h : 2 * h])
    rest = g_ref[2 * h :] - hdot(u12, u12, 0, 0)
    u22, l22 = factor_block(rest, vals, diag)
    u_ref[:h, :h] = u11
    u_ref[:h, h:] = u12
    u_ref[h:, :h] = jnp.zeros((h, h), jnp.float32)
    u_ref[h:, h:] = u22
    l_ref[:h, :h] = l11
    l_ref[:h, h:] = jnp.zeros((h, h), jnp.float32)
    l_ref[h:, :h] = -hdot(l22, hdot(u12, l11, 0, 0))
    l_ref[h:, h:] = l22


def first_kernel(g_ref, m_ref, u_ref, b_ref, low, vals, diag):
    factor_packed(g_ref, u_ref, low, vals, diag)
    for s in range(m_ref.shape[0]):
        b_ref[s] = hdot(low[...], m_ref[s])


def second_kernel(scale, g_ref, b_ref, f_ref, o_ref, r_ref, up, low, vals, diag):
    factor_packed(g_ref, up, low, vals, diag)
    slabs, count, _ = b_ref.shape
    for s in range(slabs):
        o_ref[pl.ds(s, count, stride=slabs), :] = hdot(low[...], b_ref[s]) * scale
    r_ref[...] = hdot(up[...], f_ref[...]) / scale


def gram_packed(m_ref, pack):
    slabs, count, _ = m_ref.shape
    h = count // 2
    for part, (r, c) in enumerate(((0, 0), (0, h), (h, h))):
        total = None
        for s in range(slabs):
            term = hdot(m_ref[s, r : r + h], m_ref[s, c : c + h], 1, 1)
            total = term if total is None else total + term
        pack[part * h : (part + 1) * h] = total


def start_all(axis, count, source, target, sends, recvs):
    me = lax.axis_index(axis)
    copies = []
    for step in range(1, count):
        to = lax.rem(me + step, count)
        copy = pltpu.make_async_remote_copy(
            src_ref=source(to),
            dst_ref=target(step - 1),
            send_sem=sends.at[step - 1],
            recv_sem=recvs.at[step - 1],
            device_id={axis: to},
            device_id_type=MESH,
        )
        copy.start()
        copies.append(copy)
    return copies


def greet(axis, count):
    me = lax.axis_index(axis)
    for step in range(1, count):
        pl.semaphore_signal(
            pltpu.get_barrier_semaphore(),
            inc=1,
            device_id={axis: lax.rem(me + step, count)},
            device_id_type=MESH,
        )


def sum_all(ny, nz, pack, parts, gathered, full, s1, r1, s2, r2, s3, r3):
    rows = pack.shape[0] // nz
    my, mz = lax.axis_index("gy"), lax.axis_index("gz")

    def piece(ref, index):
        return ref.at[pl.ds(pl.multiple_of(index * rows, 8), rows)]

    copies = start_all("gz", nz, lambda to: piece(pack, to), lambda k: parts.at[k], s1, r1)
    total = pack[pl.ds(pl.multiple_of(mz * rows, 8), rows), :]
    for k, copy in enumerate(copies):
        copy.wait_recv()
        total = total + parts[k]
    gathered[my] = total
    later = start_all("gy", ny, lambda to: gathered.at[my], lambda k: gathered.at[my], s2, r2)
    for copy in later:
        copy.wait_recv()
    total = gathered[0]
    for k in range(1, ny):
        total = total + gathered[k]
    full[pl.ds(pl.multiple_of(mz * rows, 8), rows), :] = total
    last = start_all("gz", nz, lambda to: piece(full, mz), lambda k: piece(full, mz), s3, r3)
    for copy in last:
        copy.wait_recv()
    for copy in copies + later + last:
        copy.wait_send()


def sum_kernel(ny, nz, m_ref, g_ref, pack, parts, gathered, full, *sems):
    greet("gy", ny)
    greet("gz", nz)
    gram_packed(m_ref, pack)
    pl.semaphore_wait(pltpu.get_barrier_semaphore(), ny + nz - 2)
    sum_all(ny, nz, pack, parts, gathered, full, *sems)
    g_ref[...] = full[...]


def sum_scratch(ny, nz, count):
    h = count // 2
    rows = 3 * h // nz
    return [
        pltpu.VMEM((3 * h, h), jnp.float32),
        pltpu.VMEM((max(nz - 1, 1), rows, h), jnp.float32),
        pltpu.VMEM((ny, rows, h), jnp.float32),
        pltpu.VMEM((3 * h, h), jnp.float32),
    ] + [pltpu.SemaphoreType.DMA((max(n - 1, 1),)) for n in (nz, nz, ny, ny, nz, nz)]


def total_gram(matrix):
    ny, nz = lax.axis_size("gy"), lax.axis_size("gz")
    count = matrix.shape[1]
    h = count // 2
    return pl.pallas_call(
        functools.partial(sum_kernel, ny, nz),
        out_shape=jax.ShapeDtypeStruct((3 * h, h), jnp.float32),
        in_specs=[VMEM],
        out_specs=VMEM,
        scratch_shapes=sum_scratch(ny, nz, count),
        compiler_params=pltpu.CompilerParams(
            collective_id=0, has_side_effects=True, vmem_limit_bytes=32 * 2**20
        ),
    )(matrix)


def first_pass(gram, matrix):
    count = matrix.shape[1]
    square = jax.ShapeDtypeStruct((count, count), jnp.float32)
    half = pltpu.VMEM((count // 2, count // 2), jnp.float32)
    return pl.pallas_call(
        first_kernel,
        out_shape=(square, jax.ShapeDtypeStruct(matrix.shape, jnp.float32)),
        in_specs=[VMEM] * 2,
        out_specs=[VMEM] * 2,
        scratch_shapes=[pltpu.VMEM((count, count), jnp.float32), half, half],
        compiler_params=pltpu.CompilerParams(vmem_limit_bytes=32 * 2**20),
    )(gram, matrix)


def second_pass(gram, basis, first, scale):
    slabs, count, lanes = basis.shape
    square = jax.ShapeDtypeStruct((count, count), jnp.float32)
    half = pltpu.VMEM((count // 2, count // 2), jnp.float32)
    whole = pltpu.VMEM((count, count), jnp.float32)
    return pl.pallas_call(
        functools.partial(second_kernel, scale),
        out_shape=(jax.ShapeDtypeStruct((count * slabs, lanes), jnp.float32), square),
        in_specs=[VMEM] * 3,
        out_specs=[VMEM] * 2,
        scratch_shapes=[whole, whole, half, half],
        compiler_params=pltpu.CompilerParams(vmem_limit_bytes=32 * 2**20),
    )(gram, basis, first)


def body(snapshots, fluid_mask):
    cells_y = snapshots.shape[1]
    cells_z = snapshots.shape[2]
    slabs = jnp.transpose(snapshots, (1, 2, 0, 3))
    extended = with_halo(slabs, (("gy", 0),), 2)
    field = filter_inner(filter_edge(extended.astype(jnp.float32), 3), 0, cells_y)
    widened = with_halo(field, (("gz", 1),), 2)
    field = filter_inner(widened, 1, cells_z)
    field = field * fluid_mask.astype(jnp.float32)[:, :, None]
    matrix = field.reshape((-1,) + field.shape[2:])
    cells = matrix.shape[0] * matrix.shape[2]
    scale = math.sqrt(cells * lax.axis_size("gy") * lax.axis_size("gz"))
    first, basis = first_pass(total_gram(matrix), matrix)
    modes, factor = second_pass(total_gram(basis), basis, first, scale)
    return (modes.reshape(snapshots.shape), factor)


def solution(mesh):
    placed = (P("grp", "gy", "gz", None), P(("grp", "gy"), "gz", None))
    return jax.shard_map(
        body,
        mesh=mesh,
        in_specs=placed,
        out_specs=(P("grp", "gy", "gz", None), P("grp", None)),
        check_vma=False,
    )
```

```python
import functools
import math

import jax
import jax.numpy as jnp
from jax import lax
from jax.experimental import pallas as pl
from jax.experimental.pallas import tpu as pltpu
from jax.sharding import PartitionSpec as P

MESH = pl.DeviceIdType.MESH
VMEM = pl.BlockSpec(memory_space=pltpu.VMEM)
gauss_taps = (0.05448868, 0.24420134, 0.40261995, 0.24420134, 0.05448868)


def lane_filter(value):
    lanes = lax.broadcasted_iota(jnp.int32, value.shape, 1)
    size = value.shape[1]
    total = gauss_taps[2] * value
    for offset in (-2, -1, 1, 2):
        moved = pltpu.roll(value, (-offset) % size, 1)
        kept = (lanes + offset >= 0) & (lanes + offset < size)
        total = total + gauss_taps[offset + 2] * jnp.where(kept, moved, 0.0)
    return total


def filter_kernel(ny, nz, s_ref, k_ref, m_ref, low, high, wide, field, sends, recvs):
    cy, cz, count, size = s_ref.shape
    my, mz = lax.axis_index("gy"), lax.axis_index("gz")
    sides = (
        (my > 0, {"gy": lax.rem(my + ny - 1, ny)}),
        (my < ny - 1, {"gy": lax.rem(my + 1, ny)}),
        (mz > 0, {"gz": lax.rem(mz + nz - 1, nz)}),
        (mz < nz - 1, {"gz": lax.rem(mz + 1, nz)}),
    )
    moves = (
        (s_ref.at[0:2], high),
        (s_ref.at[cy - 2 : cy], low),
        (field.at[:, 2:4], field.at[:, cz + 2 : cz + 4]),
        (field.at[:, cz : cz + 2], field.at[:, 0:2]),
    )

    def copy_of(k):
        return pltpu.make_async_remote_copy(
            src_ref=moves[k][0],
            dst_ref=moves[k][1],
            send_sem=sends.at[k],
            recv_sem=recvs.at[k],
            device_id=sides[k][1],
            device_id_type=MESH,
        )

    barrier = pltpu.get_barrier_semaphore()
    greeted = jnp.int32(0)
    for there, device in sides:
        greeted = greeted + jnp.where(there, jnp.int32(1), jnp.int32(0))

        @pl.when(there)
        def _():
            pl.semaphore_signal(barrier, inc=1, device_id=device, device_id_type=MESH)

    pl.semaphore_wait(barrier, greeted)
    for k in (0, 1):

        @pl.when(sides[k][0])
        def _():
            copy_of(k).start()

    def fill(source, layers, first):
        @pl.loop(0, layers * cz)
        def _(index):
            y, z = index // cz, index % cz
            wide[first + y, z] = lane_filter(source[y, z].astype(jnp.float32))

    def receive(k, there, source, first):
        @pl.when(there)
        def _():
            copy_of(k).wait_recv()
            fill(source, 2, first)

        @pl.when(jnp.logical_not(there))
        def _():
            wide[first : first + 2] = jnp.zeros((2, cz, count, size), jnp.float32)

    fill(s_ref, cy, 2)
    receive(1, my > 0, low, 0)
    receive(0, my < ny - 1, high, cy + 2)

    @pl.loop(0, cy * cz)
    def _(index):
        y, z = index // cz, index % cz
        total = gauss_taps[0] * wide[y, z]
        for offset in range(1, 5):
            total = total + gauss_taps[offset] * wide[y + offset, z]
        field[y, z + 2] = total

    for k in (2, 3):

        @pl.when(sides[k][0])
        def _():
            copy_of(k).start()

    for k, there, first in ((3, mz > 0, 0), (2, mz < nz - 1, cz + 2)):

        @pl.when(there)
        def _():
            copy_of(k).wait_recv()

        @pl.when(jnp.logical_not(there))
        def _():
            field[:, first : first + 2] = jnp.zeros((cy, 2, count, size), jnp.float32)

    @pl.loop(0, cy * cz)
    def _(index):
        y, z = index // cz, index % cz
        total = gauss_taps[0] * field[y, z]
        for offset in range(1, 5):
            total = total + gauss_taps[offset] * field[y, z + offset]
        m_ref[index] = total * k_ref[index]

    for k in range(4):

        @pl.when(sides[k][0])
        def _():
            copy_of(k).wait_send()


def filtered(slabs, mask):
    cy, cz, count, size = slabs.shape
    return pl.pallas_call(
        functools.partial(filter_kernel, lax.axis_size("gy"), lax.axis_size("gz")),
        out_shape=jax.ShapeDtypeStruct((cy * cz, count, size), jnp.float32),
        in_specs=[VMEM] * 2,
        out_specs=VMEM,
        scratch_shapes=[
            pltpu.VMEM((2, cz, count, size), slabs.dtype),
            pltpu.VMEM((2, cz, count, size), slabs.dtype),
            pltpu.VMEM((cy + 4, cz, count, size), jnp.float32),
            pltpu.VMEM((cy, cz + 4, count, size), jnp.float32),
            pltpu.SemaphoreType.DMA((4,)),
            pltpu.SemaphoreType.DMA((4,)),
        ],
        compiler_params=pltpu.CompilerParams(
            collective_id=1, has_side_effects=True, vmem_limit_bytes=32 * 2**20
        ),
    )(slabs, mask)


def hdot(a, b, ca=1, cb=0):
    return lax.dot_general(
        a,
        b,
        (((ca,), (cb,)), ((), ())),
        precision=lax.Precision.HIGHEST,
        preferred_element_type=jnp.float32,
    )


def factor_block(block, vals, diag):
    count = block.shape[0]
    lanes = lax.broadcasted_iota(jnp.int32, (8, count), 1)
    subs = lax.broadcasted_iota(jnp.int32, (8, count), 0)
    wide = (8, count)
    tiles = [block[8 * t : 8 * t + 8] for t in range(count // 8)]
    for p in range(count // 8):
        base = 8 * p
        panel = tiles[p]
        rows = [jnp.broadcast_to(panel[k : k + 1], wide) for k in range(8)]
        a = [
            [jnp.broadcast_to(rows[i][:, base + k : base + k + 1], wide) for k in range(i + 1)]
            for i in range(8)
        ]
        inv = []
        m = [[None] * 8 for _ in range(8)]
        for k in range(8):
            inv.append(1.0 / a[k][k])
            for i in range(k + 1, 8):
                m[i][k] = a[i][k] * inv[k]
            for i in range(k + 1, 8):
                for l in range(k + 1, i + 1):
                    a[i][l] = a[i][l] - m[i][k] * a[l][k]
        here = [lanes == base + k for k in range(8)]
        solved = []
        ones = []
        for i in range(8):
            row = rows[i]
            for k in range(i):
                row = jnp.where(here[k], 0.0, row) - m[i][k] * ones[k]
            solved.append(row)
            ones.append(jnp.where(here[i], 1.0, row))
        out = solved[0]
        dia = a[0][0]
        for k in range(1, 8):
            out = jnp.where(subs == k, solved[k], out)
            dia = jnp.where(subs == k, a[k][k], dia)
        vals[base : base + 8] = out
        diag[base : base + 8] = dia
        inside = (lanes >= base) & (lanes < base + 8)
        past = [jnp.where(inside & (lanes > base + k), 0.0, ones[k]) for k in range(8)]
        for t in range(p + 1, count // 8):
            tile = tiles[t]
            q = []
            for k in range(8):
                c = jnp.broadcast_to(tile[:, base + k : base + k + 1], wide)
                for l in range(k):
                    c = c - q[l] * a[k][l]
                q.append(c * inv[k])
            tile = jnp.where(inside, 0.0, tile)
            for k in range(8):
                tile = tile - q[k] * past[k]
            tiles[t] = tile
    v = vals[...]
    d = diag[...]
    s = lax.rsqrt(d)
    s = s * (1.5 - 0.5 * d * s * s)
    v = v * s
    ri = lax.broadcasted_iota(jnp.int32, (count, count), 0)
    ci = lax.broadcasted_iota(jnp.int32, (count, count), 1)
    upper = jnp.where(ci >= ri, v, 0.0)
    lower = jnp.where(ci < ri, v, jnp.where(ci == ri, s, 0.0))
    return upper, lower


def factor_packed(g_ref, u_ref, l_ref, vals, diag):
    h = g_ref.shape[1]
    u11, l11 = factor_block(g_ref[:h], vals, diag)
    u12 = hdot(l11, g_ref[h : 2 * h])
    rest = g_ref[2 * h :] - hdot(u12, u12, 0, 0)
    u22, l22 = factor_block(rest, vals, diag)
    u_ref[:h, :h] = u11
    u_ref[:h, h:] = u12
    u_ref[h:, :h] = jnp.zeros((h, h), jnp.float32)
    u_ref[h:, h:] = u22
    l_ref[:h, :h] = l11
    l_ref[:h, h:] = jnp.zeros((h, h), jnp.float32)
    l_ref[h:, :h] = -hdot(l22, hdot(u12, l11, 0, 0))
    l_ref[h:, h:] = l22


def first_kernel(g_ref, m_ref, u_ref, b_ref, low, vals, diag):
    factor_packed(g_ref, u_ref, low, vals, diag)
    for s in range(m_ref.shape[0]):
        b_ref[s] = hdot(low[...], m_ref[s])


def second_kernel(scale, g_ref, b_ref, f_ref, o_ref, r_ref, up, low, vals, diag):
    factor_packed(g_ref, up, low, vals, diag)
    slabs, count, _ = b_ref.shape
    for s in range(slabs):
        o_ref[pl.ds(s, count, stride=slabs), :] = hdot(low[...], b_ref[s]) * scale
    r_ref[...] = hdot(up[...], f_ref[...]) / scale


def gram_packed(m_ref, pack):
    slabs, count, _ = m_ref.shape
    h = count // 2
    for part, (r, c) in enumerate(((0, 0), (0, h), (h, h))):
        total = None
        for s in range(slabs):
            term = hdot(m_ref[s, r : r + h], m_ref[s, c : c + h], 1, 1)
            total = term if total is None else total + term
        pack[part * h : (part + 1) * h] = total


def start_all(axis, count, source, target, sends, recvs):
    me = lax.axis_index(axis)
    copies = []
    for step in range(1, count):
        to = lax.rem(me + step, count)
        copy = pltpu.make_async_remote_copy(
            src_ref=source(to),
            dst_ref=target(step - 1),
            send_sem=sends.at[step - 1],
            recv_sem=recvs.at[step - 1],
            device_id={axis: to},
            device_id_type=MESH,
        )
        copy.start()
        copies.append(copy)
    return copies


def greet(axis, count):
    me = lax.axis_index(axis)
    for step in range(1, count):
        pl.semaphore_signal(
            pltpu.get_barrier_semaphore(),
            inc=1,
            device_id={axis: lax.rem(me + step, count)},
            device_id_type=MESH,
        )


def sum_all(ny, nz, pack, parts, gathered, full, s1, r1, s2, r2, s3, r3):
    rows = pack.shape[0] // nz
    my, mz = lax.axis_index("gy"), lax.axis_index("gz")

    def piece(ref, index):
        return ref.at[pl.ds(pl.multiple_of(index * rows, 8), rows)]

    copies = start_all("gz", nz, lambda to: piece(pack, to), lambda k: parts.at[k], s1, r1)
    total = pack[pl.ds(pl.multiple_of(mz * rows, 8), rows), :]
    for k, copy in enumerate(copies):
        copy.wait_recv()
        total = total + parts[k]
    gathered[my] = total
    later = start_all("gy", ny, lambda to: gathered.at[my], lambda k: gathered.at[my], s2, r2)
    for copy in later:
        copy.wait_recv()
    total = gathered[0]
    for k in range(1, ny):
        total = total + gathered[k]
    full[pl.ds(pl.multiple_of(mz * rows, 8), rows), :] = total
    last = start_all("gz", nz, lambda to: piece(full, mz), lambda k: piece(full, mz), s3, r3)
    for copy in last:
        copy.wait_recv()
    for copy in copies + later + last:
        copy.wait_send()


def sum_kernel(ny, nz, m_ref, g_ref, pack, parts, gathered, full, *sems):
    greet("gy", ny)
    greet("gz", nz)
    gram_packed(m_ref, pack)
    pl.semaphore_wait(pltpu.get_barrier_semaphore(), ny + nz - 2)
    sum_all(ny, nz, pack, parts, gathered, full, *sems)
    g_ref[...] = full[...]


def sum_scratch(ny, nz, count):
    h = count // 2
    rows = 3 * h // nz
    return [
        pltpu.VMEM((3 * h, h), jnp.float32),
        pltpu.VMEM((max(nz - 1, 1), rows, h), jnp.float32),
        pltpu.VMEM((ny, rows, h), jnp.float32),
        pltpu.VMEM((3 * h, h), jnp.float32),
    ] + [pltpu.SemaphoreType.DMA((max(n - 1, 1),)) for n in (nz, nz, ny, ny, nz, nz)]


def total_gram(matrix):
    ny, nz = lax.axis_size("gy"), lax.axis_size("gz")
    count = matrix.shape[1]
    h = count // 2
    return pl.pallas_call(
        functools.partial(sum_kernel, ny, nz),
        out_shape=jax.ShapeDtypeStruct((3 * h, h), jnp.float32),
        in_specs=[VMEM],
        out_specs=VMEM,
        scratch_shapes=sum_scratch(ny, nz, count),
        compiler_params=pltpu.CompilerParams(
            collective_id=0, has_side_effects=True, vmem_limit_bytes=32 * 2**20
        ),
    )(matrix)


def first_pass(gram, matrix):
    count = matrix.shape[1]
    square = jax.ShapeDtypeStruct((count, count), jnp.float32)
    half = pltpu.VMEM((count // 2, count // 2), jnp.float32)
    return pl.pallas_call(
        first_kernel,
        out_shape=(square, jax.ShapeDtypeStruct(matrix.shape, jnp.float32)),
        in_specs=[VMEM] * 2,
        out_specs=[VMEM] * 2,
        scratch_shapes=[pltpu.VMEM((count, count), jnp.float32), half, half],
        compiler_params=pltpu.CompilerParams(vmem_limit_bytes=32 * 2**20),
    )(gram, matrix)


def second_pass(gram, basis, first, scale):
    slabs, count, lanes = basis.shape
    square = jax.ShapeDtypeStruct((count, count), jnp.float32)
    half = pltpu.VMEM((count // 2, count // 2), jnp.float32)
    whole = pltpu.VMEM((count, count), jnp.float32)
    return pl.pallas_call(
        functools.partial(second_kernel, scale),
        out_shape=(jax.ShapeDtypeStruct((count * slabs, lanes), jnp.float32), square),
        in_specs=[VMEM] * 3,
        out_specs=[VMEM] * 2,
        scratch_shapes=[whole, whole, half, half],
        compiler_params=pltpu.CompilerParams(vmem_limit_bytes=32 * 2**20),
    )(gram, basis, first)


def body(snapshots, fluid_mask):
    slabs = jnp.transpose(snapshots, (1, 2, 0, 3))
    mask = fluid_mask.astype(jnp.float32).reshape(-1, 1, fluid_mask.shape[2])
    matrix = filtered(slabs, mask)
    cells = matrix.shape[0] * matrix.shape[2]
    scale = math.sqrt(cells * lax.axis_size("gy") * lax.axis_size("gz"))
    first, basis = first_pass(total_gram(matrix), matrix)
    modes, factor = second_pass(total_gram(basis), basis, first, scale)
    return (modes.reshape(snapshots.shape), factor)


def solution(mesh):
    placed = (P("grp", "gy", "gz", None), P(("grp", "gy"), "gz", None))
    return jax.shard_map(
        body,
        mesh=mesh,
        in_specs=placed,
        out_specs=(P("grp", "gy", "gz", None), P("grp", None)),
        check_vma=False,
    )
```
